512 devices in a mesh: dp: 128 (over z_lo, x, y), layer: 4 (over z_hi, core).
Axes of the slice: x: 4, y: 4, z: 16 (z_hi: 2, z_lo: 8; z = z_hi * 8 + z_lo), core: 2. Of those that a mesh axis runs over, the one named last changes fastest.
Arguments:
- train_grads: bfloat16 [4, 65536, 4096], P('layer', 'dp'), may hold values from -0.079589844 to 0.079589844
- query_grads: bfloat16 [4, 1024, 4096], P('layer', 'dp'), may hold values from -6 to 6
- left_factor: float32 [4, 64, 64], P('layer'), may hold values from -0.12 to 2.12, as said below
- right_factor: float32 [4, 64, 64], P('layer'), may hold values from -0.12 to 2.12, as said below
Outputs:
- scores: float32 [1024, 65536], P(None, ('dp', 'layer'))
The draws below stay inside these ranges and needn't reach their ends.
Inputs may be any that keep to these rules, and one draw needn't show every extreme that they name: `left_factor`: symmetric; diagonal entries between 0.88 and 2.12, off-diagonal entries between -0.12 and 0.12. `right_factor`: symmetric; diagonal entries between 0.88 and 2.12, off-diagonal entries between -0.12 and 0.12.
All inputs are finite; a program needn't handle non-finite values.
Results may differ from the reference program's by a relative error of at most 0.0029.
Values may be sent and summed in bfloat16 or wider, within the bound.
No kernel may reach another device: no remote copies, remote signals or barrier semaphores. Data moves between devices by JAX's collectives and lax.ppermute only.
A program may use at most 128 MiB of HBM per device.

```python
import jax
import jax.numpy as jnp
from jax import lax

R = 64
D = 4096
G = 4
N = 65536
Q = 1024


def factor_matrix(key):
    diag_key, off_key = jax.random.split(key)
    diag_vals = jax.random.uniform(diag_key, (G, R), jnp.float32, 1.0, 2.0)
    noise = jax.random.uniform(off_key, (G, R, R), jnp.float32, -0.12, 0.12)
    sym_noise = 0.5 * (noise + jnp.swapaxes(noise, 1, 2))
    eye_mask = jnp.eye(R, dtype=jnp.float32)
    return sym_noise + eye_mask[None, :, :] * diag_vals[:, :, None]


def draw_left_factor(key, part):
    key = jax.random.fold_in(key, 11)
    return factor_matrix(key)


def draw_right_factor(key, part):
    key = jax.random.fold_in(key, 23)
    return factor_matrix(key)


def level_of(stream_key, dims, pieces, low, largest):
    gain = 1.0
    for position, blocks in pieces:
        steps = jax.random.uniform(jax.random.fold_in(jax.random.fold_in(stream_key, 6), position), (blocks,), jnp.float32, low / len(pieces), largest / len(pieces))
        gain = gain * jnp.repeat(jnp.exp(steps), dims[position] // blocks).reshape((-1,) + (1,) * (len(dims) - 1 - position))
    return gain


def centred(stream_key, shape, deviation, bound, pieces=(), kind=jnp.bfloat16):
    entries = jax.random.normal(stream_key, shape, jnp.float32) * deviation
    if len(pieces) > 0:
        entries = level_of(stream_key, shape, pieces, -0.22, 0.18) * entries
    return jnp.clip(entries, min=-bound, max=bound).astype(kind)


def setup_inputs(seed: int = 0) -> dict:
    key_of = jax.random.split(jax.random.key(seed), 5)
    train_grads = centred(key_of[0], (G, N, D), 0.01, 0.079589844, ((0, 4), (1, 128)))
    query_grads = centred(key_of[1], (G, Q, D), 1.0, 6.0, ((0, 4), (1, 128)))
    left_factor = draw_left_factor(jax.random.fold_in(key_of[4], 71), 0)
    right_factor = draw_right_factor(jax.random.fold_in(key_of[4], 71), 0)
    return dict(train_grads=train_grads, query_grads=query_grads, left_factor=left_factor, right_factor=right_factor)


def condition(block, left, right):
    rows = block.shape[0]
    grid = block.astype(jnp.float32).reshape(rows, R, R)
    inner = jnp.einsum("ab,qbc->qac", left, grid, precision=lax.Precision.HIGHEST)
    outer = jnp.einsum("qac,cd->qad", inner, right, precision=lax.Precision.HIGHEST)
    return outer.reshape(rows, R * R).astype(jnp.bfloat16)


def reference(train_grads, query_grads, left_factor, right_factor):
    total = jnp.zeros((Q, N), jnp.float32)
    for group in range(G):
        conditioned = condition(query_grads[group], left_factor[group], right_factor[group])
        partial_scores = lax.dot_general(conditioned, train_grads[group], (((1,), (1,)), ((), ())), preferred_element_type=jnp.float32)
        total = total + partial_scores
    return total
```

```python
import jax
import jax.numpy as jnp
from jax import lax
from jax.experimental import pallas as pl
from jax.experimental.pallas import tpu as pltpu
from jax.sharding import Mesh
from jax.sharding import PartitionSpec as P

AXES = ("z", "x", "y", "half", "core")
SIZES = (8, 4, 4, 2, 2)
RING = 4


def condition(block, left, right):
    rows = block.shape[0]
    side = left.shape[0]
    grid = block.astype(jnp.float32).reshape(rows, side, side)
    inner = jnp.einsum("ab,qbc->qac", left, grid, precision=lax.Precision.HIGHEST)
    outer = jnp.einsum("qac,cd->qad", inner, right, precision=lax.Precision.HIGHEST)
    return outer.reshape(rows, side * side).astype(jnp.bfloat16)


def moved(piece, axis, step):
    rows, owners = piece
    came = lax.ppermute(rows, axis, [(i, (i + step) % RING) for i in range(RING)])
    dx, dy = (-step, 0) if axis == "x" else (0, -step)
    return came, [(z, (x + dx) % RING, (y + dy) % RING) for z, x, y in owners]


def part(piece, start, stop):
    rows, owners = piece
    size = rows.shape[0] // len(owners)
    return rows[start * size : stop * size], owners[start:stop]


def joined(pieces):
    return jnp.concatenate([p[0] for p in pieces], 0), [o for p in pieces for o in p[1]]


def round_ring(piece, axis):
    half = len(piece[1]) // 2
    low = moved(piece, axis, 1)
    high = moved(piece, axis, -1)
    far_low = moved(part(low, 0, half), axis, 1)
    far_high = moved(part(high, half, 2 * half), axis, -1)
    return low, high, joined([far_low, far_high])


def over_plane(piece, first, second):
    low, high, far = round_ring(piece, first)
    line = joined([piece, low, high, far])
    return (line,) + round_ring(line, second)


def flipped(piece, bit):
    rows, owners = piece
    came = lax.ppermute(rows, "z", [(i, i ^ bit) for i in range(SIZES[0])])
    return came, [(z ^ bit, x, y) for z, x, y in owners]


def place_kernel(place_ref, *refs):
    count = (len(refs) - 2) // 2
    out_ref, total = refs[-2], refs[-1]
    first = 0
    for own_ref, came_ref in zip(refs[:count], refs[count : 2 * count]):
        rows = own_ref.shape[0]
        total[first : first + rows, :] = own_ref[...] + came_ref[...].astype(jnp.float32)
        first += rows
    group = out_ref.shape[0] // place_ref.shape[0]

    def step(k, carry):
        source = pl.ds(pl.multiple_of(k * group, group), group)
        target = pl.ds(pl.multiple_of(place_ref[k] * group, group), group)
        out_ref[target, :] = total[source, :]
        return carry

    lax.fori_loop(0, place_ref.shape[0], step, 0, unroll=8)


def place(own, came, places):
    rows = sum(a.shape[0] for a in own)
    shape = (rows, own[0].shape[1])
    vmem = pl.BlockSpec(memory_space=pltpu.VMEM)
    return pl.pallas_call(
        place_kernel,
        out_shape=jax.ShapeDtypeStruct(shape, jnp.float32),
        in_specs=[pl.BlockSpec(memory_space=pltpu.SMEM)] + [vmem] * (2 * len(own)),
        out_specs=vmem,
        scratch_shapes=[pltpu.VMEM(shape, jnp.float32)],
        compiler_params=pltpu.CompilerParams(vmem_limit_bytes=8 * 2**20),
    )(places, *own, *came)


def on_device(train_grads, query_grads, left_factor, right_factor):
    half, core = lax.axis_index("half"), lax.axis_index("core")
    width = train_grads.shape[1] // 4
    shares = train_grads[0].reshape(4, width, train_grads.shape[2])
    order = [2 * half + core, 2 * (1 - half) + core, 2 * half + 1 - core, 2 * (1 - half) + 1 - core]
    resident = jnp.concatenate([lax.dynamic_index_in_dim(shares, k, 0, False) for k in order], 0)

    own = condition(query_grads[0], left_factor[0], right_factor[0]), [(0, 0, 0)]
    four = flipped(own, 4)
    pair = joined([own, four])
    two = flipped(pair, 2)
    one = flipped(joined([pair, two]), 1)
    a = over_plane(pair, "y", "x")
    b = over_plane(two, "x", "y")
    c = over_plane(part(one, 0, 2), "y", "x")
    d = over_plane(part(one, 2, 4), "x", "y")
    groups = [joined([a[0], b[0], a[1], a[2]]), joined([b[1], b[2], a[3], b[3]])]
    groups += [joined([c[0], d[0], c[1], c[2]]), joined([d[1], d[2], c[3], d[3]])]

    kept, arrived, owners = [], [], []
    for rows, of in groups:
        partial_scores = lax.dot_general(
            rows, resident, (((1,), (1,)), ((), ())), preferred_element_type=jnp.float32
        )
        other = lax.ppermute(partial_scores[:, 2 * width :], "core", [(0, 1), (1, 0)])
        both = partial_scores[:, : 2 * width] + other
        kept.append(both[:, :width])
        arrived.append(lax.ppermute(both[:, width:].astype(jnp.bfloat16), "half", [(0, 1), (1, 0)]))
        owners += of
    z, x, y = (lax.axis_index(name) for name in "zxy")
    flips, dx, dy = (jnp.array([o[i] for o in owners], jnp.int32) for i in range(3))
    places = ((z ^ flips) * 4 + (x + dx) % 4) * 4 + (y + dy) % 4
    return place(kept, arrived, places.astype(jnp.int32))


def solution(mesh):
    fine = Mesh(mesh.devices.reshape(SIZES), AXES)
    dp, layer = ("z", "x", "y"), ("half", "core")
    return jax.shard_map(
        on_device,
        mesh=fine,
        in_specs=(P(layer, dp, None), P(layer, dp, None), P(layer, None, None), P(layer, None, None)),
        out_specs=P(None, dp + layer),
        check_vma=False,
    )
```

```python
import jax
import jax.numpy as jnp
from jax import lax
from jax.experimental import pallas as pl
from jax.experimental.pallas import tpu as pltpu
from jax.sharding import Mesh
from jax.sharding import PartitionSpec as P

AXES = ("z", "x", "y", "half", "core")
SIZES = (8, 4, 4, 2, 2)


def condition(block, left, right):
    rows = block.shape[0]
    side = left.shape[0]
    grid = block.astype(jnp.float32).reshape(rows, side, side)
    inner = jnp.einsum("ab,qbc->qac", left, grid, precision=lax.Precision.HIGHEST)
    outer = jnp.einsum("qac,cd->qad", inner, right, precision=lax.Precision.HIGHEST)
    return outer.reshape(rows, side * side).astype(jnp.bfloat16)


def joined(pieces):
    return jnp.concatenate([p[0] for p in pieces], 0), [o for p in pieces for o in p[1]]


def flipped(piece, bit):
    rows, owners = piece
    came = lax.ppermute(rows, "z", [(i, i ^ bit) for i in range(SIZES[0])])
    return came, [z ^ bit for z in owners]


def place_kernel(place_ref, *refs):
    count = (len(refs) - 2) // 2
    out_ref, total = refs[-2], refs[-1]
    first = 0
    for own_ref, came_ref in zip(refs[:count], refs[count : 2 * count]):
        rows = own_ref.shape[0]
        total[first : first + rows, :] = own_ref[...] + came_ref[...].astype(jnp.float32)
        first += rows
    group = out_ref.shape[0] // place_ref.shape[0]

    def step(k, carry):
        source = pl.ds(pl.multiple_of(k * group, group), group)
        target = pl.ds(pl.multiple_of(place_ref[k] * group, group), group)
        out_ref[target, :] = total[source, :]
        return carry

    lax.fori_loop(0, place_ref.shape[0], step, 0, unroll=8)


def place(own, came, places):
    rows = sum(a.shape[0] for a in own)
    shape = (rows, own[0].shape[1])
    vmem = pl.BlockSpec(memory_space=pltpu.VMEM)
    return pl.pallas_call(
        place_kernel,
        out_shape=jax.ShapeDtypeStruct(shape, jnp.float32),
        in_specs=[pl.BlockSpec(memory_space=pltpu.SMEM)] + [vmem] * (2 * len(own)),
        out_specs=vmem,
        scratch_shapes=[pltpu.VMEM(shape, jnp.float32)],
        compiler_params=pltpu.CompilerParams(vmem_limit_bytes=8 * 2**20),
    )(places, *own, *came)


def on_device(train_grads, query_grads, left_factor, right_factor):
    half, core = lax.axis_index("half"), lax.axis_index("core")
    width = train_grads.shape[1] // 4
    shares = train_grads[0].reshape(4, width, train_grads.shape[2])
    order = [2 * half + core, 2 * (1 - half) + core, 2 * half + 1 - core, 2 * (1 - half) + 1 - core]
    resident = jnp.concatenate([lax.dynamic_index_in_dim(shares, k, 0, False) for k in order], 0)

    own = condition(query_grads[0], left_factor[0], right_factor[0]), [0]
    pair = joined([own, flipped(own, 4)])
    four = joined([pair, flipped(pair, 2)])
    column, flips = joined([four, flipped(four, 1)])
    plane = lax.all_gather(column, ("x", "y"), axis=0, tiled=True)
    groups = [plane[: plane.shape[0] // 4], plane[plane.shape[0] // 4 :]]

    kept, arrived = [], []
    for rows in groups:
        partial_scores = lax.dot_general(
            rows, resident, (((1,), (1,)), ((), ())), preferred_element_type=jnp.float32
        )
        other = lax.ppermute(partial_scores[:, 2 * width :], "core", [(0, 1), (1, 0)])
        both = partial_scores[:, : 2 * width] + other
        kept.append(both[:, :width])
        arrived.append(lax.ppermute(both[:, width:].astype(jnp.bfloat16), "half", [(0, 1), (1, 0)]))
    z = lax.axis_index("z") ^ jnp.array(flips, jnp.int32)
    in_plane = lax.broadcasted_iota(jnp.int32, (16, 1), 0)
    places = (z[None, :] * 16 + in_plane).reshape(-1)
    return place(kept, arrived, places)


def solution(mesh):
    fine = Mesh(mesh.devices.reshape(SIZES), AXES)
    dp, layer = ("z", "x", "y"), ("half", "core")
    return jax.shard_map(
        on_device,
        mesh=fine,
        in_specs=(P(layer, dp, None), P(layer, dp, None), P(layer, None, None), P(layer, None, None)),
        out_specs=P(None, dp + layer),
        check_vma=False,
    )
```

```python
import jax
import jax.numpy as jnp
from jax import lax
from jax.experimental import pallas as pl
from jax.experimental.pallas import tpu as pltpu
from jax.sharding import Mesh
from jax.sharding import PartitionSpec as P

AXES = ("z", "x", "y", "half", "core")
SIZES = (8, 4, 4, 2, 2)
TURNS = (("x", 1), ("y", 1), ("x", 3), ("y", 3))


def condition(block, left, right):
    rows = block.shape[0]
    side = left.shape[0]
    grid = block.astype(jnp.float32).reshape(rows, side, side)
    inner = jnp.einsum("ab,qbc->qac", left, grid, precision=lax.Precision.HIGHEST)
    outer = jnp.einsum("qac,cd->qad", inner, right, precision=lax.Precision.HIGHEST)
    return outer.reshape(rows, side * side).astype(jnp.bfloat16)


def joined(pieces):
    rows = lax.optimization_barrier(jnp.concatenate([p[0] for p in pieces], 0))
    return rows, [o for p in pieces for o in p[1]]


def partner(piece, axis, bits):
    rows, owners = piece
    came = lax.ppermute(rows, axis, [(i, i ^ bits) for i in range(SIZES[AXES.index(axis)])])
    flip = [bits if name == axis else 0 for name in "zxy"]
    return came, [tuple(a ^ b for a, b in zip(o, flip)) for o in owners]


def place_kernel(place_ref, *refs):
    count = (len(refs) - 2) // 2
    out_ref, total = refs[-2], refs[-1]
    first = 0
    for own_ref, came_ref in zip(refs[:count], refs[count : 2 * count]):
        rows = own_ref.shape[0]
        total[first : first + rows, :] = own_ref[...] + came_ref[...].astype(jnp.float32)
        first += rows
    group = out_ref.shape[0] // place_ref.shape[0]

    def step(k, carry):
        source = pl.ds(pl.multiple_of(k * group, group), group)
        target = pl.ds(pl.multiple_of(place_ref[k] * group, group), group)
        out_ref[target, :] = total[source, :]
        return carry

    lax.fori_loop(0, place_ref.shape[0], step, 0, unroll=8)


def place(own, came, places):
    rows = sum(a.shape[0] for a in own)
    shape = (rows, own[0].shape[1])
    vmem = pl.BlockSpec(memory_space=pltpu.VMEM)
    return pl.pallas_call(
        place_kernel,
        out_shape=jax.ShapeDtypeStruct(shape, jnp.float32),
        in_specs=[pl.BlockSpec(memory_space=pltpu.SMEM)] + [vmem] * (2 * len(own)),
        out_specs=vmem,
        scratch_shapes=[pltpu.VMEM(shape, jnp.float32)],
        compiler_params=pltpu.CompilerParams(vmem_limit_bytes=8 * 2**20),
    )(places, *own, *came)


def on_device(train_grads, query_grads, left_factor, right_factor):
    half, core = lax.axis_index("half"), lax.axis_index("core")
    width = train_grads.shape[1] // 4
    resident = train_grads[0]

    own = condition(query_grads[0], left_factor[0], right_factor[0]), [(0, 0, 0)]
    pair = joined([own, partner(own, "z", 4)])
    two = partner(pair, "z", 2)
    one = partner(pair, "z", 1)
    held = [pair, two, one, partner(two, "z", 1)]
    for step in range(len(TURNS)):
        came = [partner(p, *TURNS[(k + step) % len(TURNS)]) for k, p in enumerate(held)]
        if step < len(TURNS) - 1:
            held = [joined(pieces) for pieces in zip(held, came)]

    kept, arrived, owners = [], [], []
    for pieces in (held[:2], held[2:] + came[:1], came[1:]):
        partial_scores = jnp.concatenate(
            [
                lax.dot_general(rows, resident, (((1,), (1,)), ((), ())), preferred_element_type=jnp.float32)
                for rows, _ in pieces
            ],
            0,
        )
        shares = [partial_scores[:, k * width : (k + 1) * width] for k in range(4)]
        away = [jnp.where(core == 0, shares[2 * k + 1], shares[2 * k]) for k in range(2)]
        here = [jnp.where(core == 0, shares[2 * k], shares[2 * k + 1]) for k in range(2)]
        other = lax.ppermute(jnp.concatenate(away, 1), "core", [(0, 1), (1, 0)])
        both = [here[k] + other[:, k * width : (k + 1) * width] for k in range(2)]
        kept.append(jnp.where(half == 0, both[0], both[1]))
        cross = jnp.where(half == 0, both[1], both[0]).astype(jnp.bfloat16)
        arrived.append(lax.ppermute(cross, "half", [(0, 1), (1, 0)]))
        owners += [o for piece in pieces for o in piece[1]]
    z, x, y = (lax.axis_index(n) ^ jnp.array([o[k] for o in owners], jnp.int32) for k, n in enumerate("zxy"))
    places = (z * SIZES[1] + x) * SIZES[2] + y
    return place(kept, arrived, places)


def solution(mesh):
    fine = Mesh(mesh.devices.reshape(SIZES), AXES)
    dp, layer = ("z", "x", "y"), ("half", "core")
    return jax.shard_map(
        on_device,
        mesh=fine,
        in_specs=(P(layer, dp, None), P(layer, dp, None), P(layer, None, None), P(layer, None, None)),
        out_specs=P(None, dp + layer),
        check_vma=False,
    )
```

```python
import itertools
import math

import jax
import jax.numpy as jnp
from jax import lax
from jax.experimental import pallas as pl
from jax.experimental.pallas import tpu as pltpu
from jax.sharding import Mesh
from jax.sharding import PartitionSpec as P

AXES = ("z", "x", "y", "half", "core")
SIZES = (8, 4, 4, 2, 2)
TURNS = ((0, 1, 0), (0, 0, 1), (0, 3, 0), (0, 0, 3))


def condition(block, left, right):
    rows = block.shape[0]
    side = left.shape[0]
    grid = block.astype(jnp.float32).reshape(rows, side, side)
    inner = jnp.einsum("ab,qbc->qac", left, grid, precision=lax.Precision.HIGHEST)
    outer = jnp.einsum("qac,cd->qad", inner, right, precision=lax.Precision.HIGHEST)
    return outer.reshape(rows, side * side).astype(jnp.bfloat16)


def flipped(owners, flip):
    return [tuple(a ^ b for a, b in zip(o, flip)) for o in owners]


def sent(rows, flips):
    names = ("z", "x", "y", "core")
    sizes = tuple(SIZES[AXES.index(n)] for n in names)
    pairs = []
    for source in itertools.product(*map(range, sizes)):
        if flips[source[3]] is not None:
            target = tuple(a ^ b for a, b in zip(source, flips[source[3]] + (0,)))
            pairs.append(tuple(sum(p * math.prod(sizes[k + 1 :]) for k, p in enumerate(at)) for at in (source, target)))
    return lax.ppermute(rows, names, pairs)


def partner(piece, flips):
    return (sent(piece[0], flips),) + tuple(flipped(piece[1 + c], flips[c]) for c in range(2))


def joined(one, two):
    return lax.optimization_barrier(jnp.concatenate([one[0], two[0]], 1)), one[1] + two[1], one[2] + two[2]


def place_kernel(place_ref, *refs):
    count = (len(refs) - 2) // 2
    out_ref, total = refs[-2], refs[-1]
    first = 0
    for own_ref, came_ref in zip(refs[:count], refs[count : 2 * count]):
        rows = own_ref.shape[0]
        total[first : first + rows, :] = own_ref[...] + came_ref[...].astype(jnp.float32)
        first += rows
    group = out_ref.shape[0] // place_ref.shape[0]

    def step(k, carry):
        source = pl.ds(pl.multiple_of(k * group, group), group)
        target = pl.ds(pl.multiple_of(place_ref[k] * group, group), group)
        out_ref[target, :] = total[source, :]
        return carry

    lax.fori_loop(0, place_ref.shape[0], step, 0, unroll=8)


def place(own, came, places):
    rows = sum(a.shape[0] for a in own)
    shape = (rows, own[0].shape[1])
    vmem = pl.BlockSpec(memory_space=pltpu.VMEM)
    return pl.pallas_call(
        place_kernel,
        out_shape=jax.ShapeDtypeStruct(shape, jnp.float32),
        in_specs=[pl.BlockSpec(memory_space=pltpu.SMEM)] + [vmem] * (2 * len(own)),
        out_specs=vmem,
        scratch_shapes=[pltpu.VMEM(shape, jnp.float32)],
        compiler_params=pltpu.CompilerParams(vmem_limit_bytes=8 * 2**20),
    )(places, *own, *came)


def on_device(train_grads, query_grads, left_factor, right_factor):
    half, core = lax.axis_index("half"), lax.axis_index("core")
    width = train_grads.shape[1] // 4
    swap = [(0, 1), (1, 0)]

    own = condition(query_grads[0], left_factor[0], right_factor[0])
    pair = jnp.concatenate([own, sent(own, [(4, 0, 0)] * 2)], 0)
    both = lax.optimization_barrier(jnp.stack([pair, lax.ppermute(pair, "core", swap)]))
    first = sent(both, [(2, 0, 0), (1, 0, 0)])
    second = sent(both, [None, (3, 0, 0)])
    trains = (train_grads[0], lax.ppermute(train_grads[0], "core", swap))
    near = [(0, 0, 0), (4, 0, 0)]
    held = [
        (jnp.where(core == 0, both, first), near, flipped(near, (1, 0, 0))),
        (jnp.where(core == 0, first, second), flipped(near, (2, 0, 0)), flipped(near, (3, 0, 0))),
    ]
    for step in range(len(TURNS)):
        turn = [TURNS[(k + step) % len(TURNS)] for k in range(4)]
        came = [partner(p, turn[2 * k : 2 * k + 2]) for k, p in enumerate(held)]
        if step < len(TURNS) - 1:
            held = [joined(*pieces) for pieces in zip(held, came)]

    kept, arrived, owners = [], [], ([], [])
    for last in (False, True):
        pieces = held[1:] + came if last else held[:1]
        scores = jnp.concatenate(
            [
                sum(
                    lax.dot_general(r, t, (((1,), (1,)), ((), ())), preferred_element_type=jnp.float32)
                    for r, t in zip(rows, trains)
                )
                for rows, _, _ in pieces
            ],
            0,
        )
        shares = [scores[:, k * width : (k + 1) * width] for k in range(4)]
        away = [jnp.where(core == 0, shares[2 * k + 1], shares[2 * k]) for k in range(2)]
        here = [jnp.where(core == 0, shares[2 * k], shares[2 * k + 1]) for k in range(2)]
        other = lax.ppermute(jnp.concatenate(away, 1), "core", swap)
        whole = [jnp.concatenate([here[k], other[:, k * width : (k + 1) * width]], 0) for k in range(2)]
        kept.append(jnp.where(half == 0, whole[0], whole[1]))
        cross = jnp.where(half == 0, whole[1], whole[0]).astype(jnp.bfloat16)
        arrived.append(lax.ppermute(cross, "half", swap))
        if not last:
            arrived[0], rows = lax.optimization_barrier((arrived[0], came[0][0]))
            came[0] = (rows,) + came[0][1:]
        for c in range(2):
            owners[c].extend(o for k in (1 + c, 2 - c) for piece in pieces for o in piece[k])
    flips = jnp.where(core == 0, jnp.array(owners[0], jnp.int32).T, jnp.array(owners[1], jnp.int32).T)
    z, x, y = (lax.axis_index(n) ^ flips[k] for k, n in enumerate("zxy"))
    places = (z * SIZES[1] + x) * SIZES[2] + y
    return place(kept, arrived, places)


def solution(mesh):
    fine = Mesh(mesh.devices.reshape(SIZES), AXES)
    dp, layer = ("z", "x", "y"), ("half", "core")
    return jax.shard_map(
        on_device,
        mesh=fine,
        in_specs=(P(layer, dp, None), P(layer, dp, None), P(layer, None, None), P(layer, None, None)),
        out_specs=P(None, dp + layer),
        check_vma=False,
    )
```

```python
import itertools
import math

import jax
import jax.numpy as jnp
from jax import lax
from jax.experimental import pallas as pl
from jax.experimental.pallas import tpu as pltpu
from jax.sharding import Mesh
from jax.sharding import PartitionSpec as P

AXES = ("z", "x", "y", "half", "core")
SIZES = (8, 4, 4, 2, 2)
TURNS = ((0, 1, 0), (0, 0, 1), (0, 3, 0), (0, 0, 3))


def condition(block, left, right):
    rows = block.shape[0]
    side = left.shape[0]
    grid = block.astype(jnp.float32).reshape(rows, side, side)
    inner = jnp.einsum("ab,qbc->qac", left, grid, precision=lax.Precision.HIGHEST)
    outer = jnp.einsum("qac,cd->qad", inner, right, precision=lax.Precision.HIGHEST)
    return outer.reshape(rows, side * side).astype(jnp.bfloat16)


def flipped(owners, flip):
    return [tuple(a ^ b for a, b in zip(o, flip)) for o in owners]


def sent(rows, flips):
    names = ("z", "x", "y", "core")
    sizes = tuple(SIZES[AXES.index(n)] for n in names)
    pairs = []
    for source in itertools.product(*map(range, sizes)):
        if flips[source[3]] is not None:
            target = tuple(a ^ b for a, b in zip(source, flips[source[3]] + (0,)))
            pairs.append(tuple(sum(p * math.prod(sizes[k + 1 :]) for k, p in enumerate(at)) for at in (source, target)))
    return lax.ppermute(rows, names, pairs)


def partner(piece, flips):
    return (sent(piece[0], flips),) + tuple(flipped(piece[1 + c], flips[c]) for c in range(2))


def joined(one, two):
    return lax.optimization_barrier(jnp.concatenate([one[0], two[0]], 1)), one[1] + two[1], one[2] + two[2]


def place_kernel(place_ref, *refs):
    count = (len(refs) - 2) // 2
    out_ref, total = refs[-2], refs[-1]
    first = 0
    for own_ref, came_ref in zip(refs[:count], refs[count : 2 * count]):
        rows = own_ref.shape[0]
        total[first : first + rows, :] = own_ref[...] + came_ref[...].astype(jnp.float32)
        first += rows
    group = out_ref.shape[0] // place_ref.shape[0]

    def step(k, carry):
        source = pl.ds(pl.multiple_of(k * group, group), group)
        target = pl.ds(pl.multiple_of(place_ref[k] * group, group), group)
        out_ref[target, :] = total[source, :]
        return carry

    lax.fori_loop(0, place_ref.shape[0], step, 0, unroll=8)


def place(own, came, places):
    rows = sum(a.shape[0] for a in own)
    shape = (rows, own[0].shape[1])
    vmem = pl.BlockSpec(memory_space=pltpu.VMEM)
    return pl.pallas_call(
        place_kernel,
        out_shape=jax.ShapeDtypeStruct(shape, jnp.float32),
        in_specs=[pl.BlockSpec(memory_space=pltpu.SMEM)] + [vmem] * (2 * len(own)),
        out_specs=vmem,
        scratch_shapes=[pltpu.VMEM(shape, jnp.float32)],
        compiler_params=pltpu.CompilerParams(vmem_limit_bytes=8 * 2**20),
    )(places, *own, *came)


def on_device(train_grads, query_grads, left_factor, right_factor):
    half, core = lax.axis_index("half"), lax.axis_index("core")
    width = train_grads.shape[1] // 4
    swap = [(0, 1), (1, 0)]

    trains = [train_grads[0], lax.ppermute(train_grads[0], "core", swap)]
    own = condition(query_grads[0], left_factor[0], right_factor[0])
    both = lax.optimization_barrier(jnp.stack([own, lax.ppermute(own, "core", swap)]))
    rows = both.shape[1]
    pair = lax.optimization_barrier(jnp.concatenate([both, sent(both, [(4, 0, 0), (1, 0, 0)])], 1))
    pair, trains[1] = lax.optimization_barrier((pair, trains[1]))
    more = sent(pair, [(2, 0, 0), (4, 0, 0)])
    first = jnp.where(core == 0, pair, jnp.concatenate([pair[:, rows:], more[:, rows:]], 1))
    first = lax.optimization_barrier(first)
    second = jnp.where(core == 0, more, sent(first, [None, (2, 0, 0)]))
    held = [
        (first, [(0, 0, 0), (4, 0, 0)], [(1, 0, 0), (5, 0, 0)]),
        (second, [(2, 0, 0), (6, 0, 0)], [(3, 0, 0), (7, 0, 0)]),
    ]
    sibling = jnp.where(core < 2, trains[1], jnp.zeros_like(trains[1]))
    trains[1] = lax.optimization_barrier(sibling)
    for step in range(len(TURNS)):
        turn = [TURNS[(k + step) % len(TURNS)] for k in range(4)]
        came = [partner(p, turn[2 * k : 2 * k + 2]) for k, p in enumerate(held)]
        if step < len(TURNS) - 1:
            held = [joined(*pieces) for pieces in zip(held, came)]

    kept, arrived, owners = [], [], ([], [])
    for last in (False, True):
        pieces = held[1:] + came if last else held[:1]
        scores = jnp.concatenate(
            [
                sum(
                    lax.dot_general(r, t, (((1,), (1,)), ((), ())), preferred_element_type=jnp.float32)
                    for r, t in zip(rows, trains)
                )
                for rows, _, _ in pieces
            ],
            0,
        )
        shares = [scores[:, k * width : (k + 1) * width] for k in range(4)]
        away = [jnp.where(core == 0, shares[2 * k + 1], shares[2 * k]) for k in range(2)]
        here = [jnp.where(core == 0, shares[2 * k], shares[2 * k + 1]) for k in range(2)]
        other = lax.ppermute(jnp.concatenate(away, 1), "core", swap)
        whole = [jnp.concatenate([here[k], other[:, k * width : (k + 1) * width]], 0) for k in range(2)]
        kept.append(jnp.where(half == 0, whole[0], whole[1]))
        cross = jnp.where(half == 0, whole[1], whole[0]).astype(jnp.bfloat16)
        arrived.append(lax.ppermute(cross, "half", swap))
        if not last:
            arrived[0], rows = lax.optimization_barrier((arrived[0], came[0][0]))
            came[0] = (rows,) + came[0][1:]
        for c in range(2):
            owners[c].extend(o for k in (1 + c, 2 - c) for piece in pieces for o in piece[k])
    flips = jnp.where(core == 0, jnp.array(owners[0], jnp.int32).T, jnp.array(owners[1], jnp.int32).T)
    z, x, y = (lax.axis_index(n) ^ flips[k] for k, n in enumerate("zxy"))
    places = (z * SIZES[1] + x) * SIZES[2] + y
    return place(kept, arrived, places)


def solution(mesh):
    fine = Mesh(mesh.devices.reshape(SIZES), AXES)
    dp, layer = ("z", "x", "y"), ("half", "core")
    return jax.shard_map(
        on_device,
        mesh=fine,
        in_specs=(P(layer, dp, None), P(layer, dp, None), P(layer, None, None), P(layer, None, None)),
        out_specs=P(None, dp + layer),
        check_vma=False,
    )
```

```python
import jax
import jax.numpy as jnp
from jax import lax
from jax.experimental import pallas as pl
from jax.experimental.pallas import tpu as pltpu
from jax.sharding import Mesh
from jax.sharding import PartitionSpec as P

AXES = ("z", "x", "y", "half", "core")
SIZES = (8, 4, 4, 2, 2)
TURNS = (("x", 1), ("y", 1), ("x", 3), ("y", 3))


def condition(block, left, right):
    rows = block.shape[0]
    side = left.shape[0]
    grid = block.astype(jnp.float32).reshape(rows, side, side)
    inner = jnp.einsum("ab,qbc->qac", left, grid, precision=lax.Precision.HIGHEST)
    outer = jnp.einsum("qac,cd->qad", inner, right, precision=lax.Precision.HIGHEST)
    return outer.reshape(rows, side * side).astype(jnp.bfloat16)


def joined(pieces):
    rows = lax.optimization_barrier(jnp.concatenate([p[0] for p in pieces], 0))
    return rows, [o for p in pieces for o in p[1]]


def partner(piece, axis, bits):
    rows, owners = piece
    came = lax.ppermute(rows, axis, [(i, i ^ bits) for i in range(SIZES[AXES.index(axis)])])
    flip = [bits if name == axis else 0 for name in "zxy"]
    return came, [tuple(a ^ b for a, b in zip(o, flip)) for o in owners]


def place_kernel(place_ref, *refs):
    count = (len(refs) - 2) // 2
    out_ref, total = refs[-2], refs[-1]
    first = 0
    for own_ref, came_ref in zip(refs[:count], refs[count : 2 * count]):
        rows = own_ref.shape[0]
        total[first : first + rows, :] = own_ref[...] + came_ref[...].astype(jnp.float32)
        first += rows
    group = out_ref.shape[0] // place_ref.shape[0]

    def step(k, carry):
        source = pl.ds(pl.multiple_of(k * group, group), group)
        target = pl.ds(pl.multiple_of(place_ref[k] * group, group), group)
        out_ref[target, :] = total[source, :]
        return carry

    lax.fori_loop(0, place_ref.shape[0], step, 0, unroll=8)


def place(own, came, places):
    rows = sum(a.shape[0] for a in own)
    shape = (rows, own[0].shape[1])
    vmem = pl.BlockSpec(memory_space=pltpu.VMEM)
    return pl.pallas_call(
        place_kernel,
        out_shape=jax.ShapeDtypeStruct(shape, jnp.float32),
        in_specs=[pl.BlockSpec(memory_space=pltpu.SMEM)] + [vmem] * (2 * len(own)),
        out_specs=vmem,
        scratch_shapes=[pltpu.VMEM(shape, jnp.float32)],
        compiler_params=pltpu.CompilerParams(vmem_limit_bytes=8 * 2**20),
    )(places, *own, *came)


def on_device(train_grads, query_grads, left_factor, right_factor):
    half, core = lax.axis_index("half"), lax.axis_index("core")
    width = train_grads.shape[1] // 4
    resident = train_grads[0]

    own = condition(query_grads[0], left_factor[0], right_factor[0]), [(0, 0, 0)]
    pair = joined([own, partner(own, "z", 4)])
    two = partner(pair, "z", 2)
    one = partner(pair, "z", 1)
    held = [pair, two, one, partner(two, "z", 1)]
    for step in range(len(TURNS)):
        came = [partner(p, *TURNS[(k + step) % len(TURNS)]) for k, p in enumerate(held)]
        if step < len(TURNS) - 1:
            held = [joined(pieces) for pieces in zip(held, came)]

    ready = lax.optimization_barrier(tuple(rows for rows, _ in held))
    held = [(rows, piece[1]) for rows, piece in zip(ready, held)]
    kept, arrived, owners = [], [], []
    for pieces in (held[:2], held[2:] + came):
        partial_scores = jnp.concatenate(
            [
                lax.dot_general(rows, resident, (((1,), (1,)), ((), ())), preferred_element_type=jnp.float32)
                for rows, _ in pieces
            ],
            0,
        )
        shares = [partial_scores[:, k * width : (k + 1) * width] for k in range(4)]
        away = [jnp.where(core == 0, shares[2 * k + 1], shares[2 * k]) for k in range(2)]
        here = [jnp.where(core == 0, shares[2 * k], shares[2 * k + 1]) for k in range(2)]
        away = jnp.concatenate(away, 1)
        if arrived:
            away, arrived[0] = lax.optimization_barrier((away, arrived[0]))
        other = lax.ppermute(away, "core", [(0, 1), (1, 0)])
        both = [here[k] + other[:, k * width : (k + 1) * width] for k in range(2)]
        kept.append(jnp.where(half == 0, both[0], both[1]))
        cross = jnp.where(half == 0, both[1], both[0]).astype(jnp.bfloat16)
        arrived.append(lax.ppermute(cross, "half", [(0, 1), (1, 0)]))
        owners += [o for piece in pieces for o in piece[1]]
    z, x, y = (lax.axis_index(n) ^ jnp.array([o[k] for o in owners], jnp.int32) for k, n in enumerate("zxy"))
    places = (z * SIZES[1] + x) * SIZES[2] + y
    return place(kept, arrived, places)


def solution(mesh):
    fine = Mesh(mesh.devices.reshape(SIZES), AXES)
    dp, layer = ("z", "x", "y"), ("half", "core")
    return jax.shard_map(
        on_device,
        mesh=fine,
        in_specs=(P(layer, dp, None), P(layer, dp, None), P(layer, None, None), P(layer, None, None)),
        out_specs=P(None, dp + layer),
        check_vma=False,
    )
```

```python
import jax
import jax.numpy as jnp
from jax import lax
from jax.experimental import pallas as pl
from jax.experimental.pallas import tpu as pltpu
from jax.sharding import Mesh
from jax.sharding import PartitionSpec as P

AXES = ("z", "x", "y", "half", "core")
SIZES = (8, 4, 4, 2, 2)
TURNS = (("x", 1), ("y", 1), ("x", 3), ("y", 3))


def condition(block, left, right):
    rows = block.shape[0]
    side = left.shape[0]
    grid = block.astype(jnp.float32).reshape(rows, side, side)
    inner = jnp.einsum("ab,qbc->qac", left, grid, precision=lax.Precision.HIGHEST)
    outer = jnp.einsum("qac,cd->qad", inner, right, precision=lax.Precision.HIGHEST)
    return outer.reshape(rows, side * side).astype(jnp.bfloat16)


def joined(pieces):
    rows = lax.optimization_barrier(jnp.concatenate([p[0] for p in pieces], 0))
    return rows, [o for p in pieces for o in p[1]]


def partner(piece, axis, bits):
    rows, owners = piece
    came = lax.ppermute(rows, axis, [(i, i ^ bits) for i in range(SIZES[AXES.index(axis)])])
    flip = [bits if name == axis else 0 for name in "zxy"]
    return came, [tuple(a ^ b for a, b in zip(o, flip)) for o in owners]


def place_kernel(place_ref, *refs):
    count = (len(refs) - 2) // 2
    out_ref, total = refs[-2], refs[-1]
    first = 0
    for own_ref, came_ref in zip(refs[:count], refs[count : 2 * count]):
        rows = own_ref.shape[0]
        total[first : first + rows, :] = own_ref[...] + came_ref[...].astype(jnp.float32)
        first += rows
    group = out_ref.shape[0] // place_ref.shape[0]

    def step(k, carry):
        source = pl.ds(pl.multiple_of(k * group, group), group)
        target = pl.ds(pl.multiple_of(place_ref[k] * group, group), group)
        out_ref[target, :] = total[source, :]
        return carry

    lax.fori_loop(0, place_ref.shape[0], step, 0, unroll=8)


def place(own, came, places):
    rows = sum(a.shape[0] for a in own)
    shape = (rows, own[0].shape[1])
    vmem = pl.BlockSpec(memory_space=pltpu.VMEM)
    return pl.pallas_call(
        place_kernel,
        out_shape=jax.ShapeDtypeStruct(shape, jnp.float32),
        in_specs=[pl.BlockSpec(memory_space=pltpu.SMEM)] + [vmem] * (2 * len(own)),
        out_specs=vmem,
        scratch_shapes=[pltpu.VMEM(shape, jnp.float32)],
        compiler_params=pltpu.CompilerParams(vmem_limit_bytes=8 * 2**20),
    )(places, *own, *came)


def on_device(train_grads, query_grads, left_factor, right_factor):
    half, core = lax.axis_index("half"), lax.axis_index("core")
    width = train_grads.shape[1] // 4
    resident = train_grads[0]

    own = condition(query_grads[0], left_factor[0], right_factor[0]), [(0, 0, 0)]
    four, two, one = (partner(own, "z", bits) for bits in (4, 2, 1))
    count = own[0].shape[0]
    rows, owners = partner(joined([two, one]), "z", 4)
    pairs = [joined([p, (rows[k * count : (k + 1) * count], owners[k : k + 1])]) for k, p in enumerate((two, one))]
    held = [joined([own, four])] + pairs + [partner(pairs[0], "z", 1)]
    for step in range(len(TURNS)):
        came = [partner(p, *TURNS[(k + step) % len(TURNS)]) for k, p in enumerate(held)]
        if step < len(TURNS) - 1:
            held = [joined(pieces) for pieces in zip(held, came)]

    ready = lax.optimization_barrier(tuple(rows for rows, _ in held))
    held = [(rows, piece[1]) for rows, piece in zip(ready, held)]
    kept, arrived, owners = [], [], []
    for pieces in (held[:2], held[2:] + came):
        partial_scores = jnp.concatenate(
            [
                lax.dot_general(rows, resident, (((1,), (1,)), ((), ())), preferred_element_type=jnp.float32)
                for rows, _ in pieces
            ],
            0,
        )
        shares = [partial_scores[:, k * width : (k + 1) * width] for k in range(4)]
        away = [jnp.where(core == 0, shares[2 * k + 1], shares[2 * k]) for k in range(2)]
        here = [jnp.where(core == 0, shares[2 * k], shares[2 * k + 1]) for k in range(2)]
        away = jnp.concatenate(away, 1)
        if arrived:
            away, arrived[0] = lax.optimization_barrier((away, arrived[0]))
        other = lax.ppermute(away, "core", [(0, 1), (1, 0)])
        both = [here[k] + other[:, k * width : (k + 1) * width] for k in range(2)]
        kept.append(jnp.where(half == 0, both[0], both[1]))
        cross = jnp.where(half == 0, both[1], both[0]).astype(jnp.bfloat16)
        arrived.append(lax.ppermute(cross, "half", [(0, 1), (1, 0)]))
        owners += [o for piece in pieces for o in piece[1]]
    z, x, y = (lax.axis_index(n) ^ jnp.array([o[k] for o in owners], jnp.int32) for k, n in enumerate("zxy"))
    places = (z * SIZES[1] + x) * SIZES[2] + y
    return place(kept, arrived, places)


def solution(mesh):
    fine = Mesh(mesh.devices.reshape(SIZES), AXES)
    dp, layer = ("z", "x", "y"), ("half", "core")
    return jax.shard_map(
        on_device,
        mesh=fine,
        in_specs=(P(layer, dp, None), P(layer, dp, None), P(layer, None, None), P(layer, None, None)),
        out_specs=P(None, dp + layer),
        check_vma=False,
    )
```
